128 devices in a mesh: group: 8 (over x, core), tp: 16 (over y, z).
Axes of the slice: x: 4, y: 4, z: 4, core: 2. Of those that a mesh axis runs over, the one named last changes fastest.
Arguments:
- prefix_store: bfloat16 [64, 128, 7168], P('group', None, 'tp'), may hold values from -6 to 6
- page_owner: int32 [16, 4], replicated, may hold values from 0 to 63, as said below
- prefix_len: int32 [16], P('group'), may hold values from 1 to 512, 6144 in all
- turn_rows: bfloat16 [16, 256, 7168], P('group', None, 'tp'), may hold values from -6 to 6
- turn_len: int32 [16], P('group'), may hold values from 1 to 256, 3072 in all
- w_query: bfloat16 [7168, 8192], P(None, 'tp'), may hold values from -0.091937622 to 0.091937622
- w_key: bfloat16 [7168, 8192], P(None, 'tp'), may hold values from -0.091937622 to 0.091937622
- w_value: bfloat16 [7168, 8192], P(None, 'tp'), may hold values from -0.0625 to 0.0625
Outputs:
- context: bfloat16 [16, 256, 8192], P('group', None, 'tp')
The draws below stay inside these ranges and needn't reach their ends.
Inputs may be any that keep to these rules, and one draw needn't show every extreme that they name: `page_owner`: each slot is named once. Slot s is held by index s // 8 of group; conversation c belongs to index c // 2. The pages of one index of group's conversations come from 4 indices of group, exactly 2 pages from each of them.
All inputs are finite; a program needn't handle non-finite values. No bound on the sum of `prefix_len` or of `turn_len` on one device may be relied on, other than what follows from the above.
Results may differ from the reference program's by a relative error of at most 0.011.
Values may be sent and summed in bfloat16 or wider, within the bound.
A program may use at most 128 MiB of HBM per device.

```python
import math
import jax
import jax.numpy as jnp
import numpy as np
from jax import lax

D = 7168
HEADS = 64
HS = 128
PREFIX = 512
TURN = 256
PAGE = 128
CONV_GRP = 2
PAGES = 4
NCONV = 16
SLOTS = 64
CAP = 2


def draw_page_owner(key, part):
    key = jax.random.fold_in(key, 11)
    groups = NCONV // CONV_GRP
    per_group = CONV_GRP * PAGES
    spread = per_group // CAP
    key_offsets, key_codes, key_slots = jax.random.split(key, 3)
    shuffled = jax.random.permutation(key_offsets, groups).astype(jnp.int32)
    positions = jnp.arange(groups, dtype=jnp.int32)
    rank = jnp.where(shuffled == groups // 2, 0, jnp.where(shuffled == groups - 1, 1, jnp.where(shuffled == 1, 2, 3 + positions)))
    offsets = shuffled[jnp.argsort(rank, stable=True)][:spread]
    codes = jax.vmap(lambda single: jax.random.permutation(single, per_group))(jax.random.split(key_codes, groups)).astype(jnp.int32)
    first_code = codes[:, 0:1]
    page_index = jnp.arange(per_group, dtype=jnp.int32)[None, :]
    page_codes = jnp.where(page_index == 0, 0, jnp.where(codes == 0, first_code, codes))
    slot_order = jax.vmap(lambda single: jax.random.permutation(single, per_group))(jax.random.split(key_slots, groups)).astype(jnp.int32)
    target = jnp.arange(groups, dtype=jnp.int32)[:, None]
    source = (target + offsets[page_codes // CAP]) % groups
    owner = source * per_group + slot_order[source, page_codes]
    return owner.reshape(NCONV, PAGES).astype(jnp.int32)


def draw_w_query(key, part):
    key = jax.random.fold_in(key, 21)
    base = jax.random.truncated_normal(key, -6.0, 6.0, (D, HEADS * HS), jnp.float32) / D ** 0.5
    return base.astype(jnp.bfloat16)


def draw_w_key(key, part):
    key = jax.random.fold_in(key, 23)
    base = jax.random.truncated_normal(key, -6.0, 6.0, (D, HEADS * HS), jnp.float32) / D ** 0.5
    return base.astype(jnp.bfloat16)


def levels(rng, extent, cuts, low, largest):
    def one(position, shards_of):
        draws = jax.random.uniform(jax.random.fold_in(jax.random.fold_in(rng, 6), position), (shards_of,), jnp.float32, low / len(cuts), largest / len(cuts))
        return jnp.repeat(jnp.exp(draws), extent[position] // shards_of).reshape((-1,) + (1,) * (len(extent) - position - 1))

    level = one(*cuts[0])
    for cut in cuts[1:]:
        level = level * one(*cut)
    return level


def length_profile(count, total, reach, slope):
    weights = [(1 << 20) // math.isqrt(standing ** slope) + 1 for standing in range(2, count + 1)]
    surplus, given = total - reach - (count - 1), [1] * (count - 1)
    while surplus > 0:
        free = [i for i in range(count - 1) if given[i] < reach]
        mass, left = sum([weights[i] for i in free]), surplus
        for i in free:
            more = min(reach - given[i], max(1, left * weights[i] // mass), surplus)
            given[i] = given[i] + more
            surplus = surplus - more
    return np.array([reach] + given)


def ragged(stream_key, count, total, limit, lean):
    if count == 2:
        one = jax.random.randint(stream_key, (), max(1, total - limit), min(limit, total - 1) + 1)
        return jnp.stack([one, total - one])
    tallies = jnp.asarray(length_profile(count, total, limit, lean), jnp.int32)
    couples = (count - 1) // 2
    source_of, sink = tallies[1:1 + 2 * couples:2], tallies[2:2 + 2 * couples:2]
    room = jnp.minimum(source_of - 1, limit - sink)
    moved = jax.random.randint(jax.random.fold_in(stream_key, 1), (couples,), 0, 1 << 20) % (room + 1)
    tallies = tallies.at[1:1 + 2 * couples:2].set(source_of - moved).at[2:2 + 2 * couples:2].set(sink + moved)
    return tallies[jax.random.permutation(jax.random.fold_in(stream_key, 2), count)]


def noise(stream_key, extent, deviation, most, cuts=(), held_as=jnp.bfloat16):
    values = deviation * jax.random.normal(stream_key, extent, jnp.float32)
    if cuts:
        values = values * levels(stream_key, extent, cuts, -0.22, 0.18)
    return jnp.clip(values, -most, most).astype(held_as)


def setup_inputs(seed: int = 0) -> dict:
    key_of = jax.random.split(jax.random.key(seed), 9)
    return {
        "prefix_store": noise(key_of[0], (SLOTS, PAGE, D), 1.0, 6.0, ((0, 8), (2, 16))),
        "page_owner": draw_page_owner(jax.random.fold_in(key_of[8], 71), 0),
        "prefix_len": ragged(key_of[2], NCONV, NCONV * PREFIX * 3 // 4, PREFIX, 1).astype(jnp.int32),
        "turn_rows": noise(key_of[3], (NCONV, TURN, D), 1.0, 6.0, ((0, 8), (2, 16))),
        "turn_len": ragged(key_of[4], NCONV, NCONV * TURN * 3 // 4, TURN, 1).astype(jnp.int32),
        "w_query": draw_w_query(jax.random.fold_in(key_of[8], 71), 0),
        "w_key": draw_w_key(jax.random.fold_in(key_of[8], 71), 0),
        "w_value": noise(key_of[7], (D, HEADS * HS), D ** -0.5, 0.0625, ((1, 16),)),
    }


first_head = 48.0
all_heads = 112.0


def alibi_slopes(head_index):
    return 2.0 ** (-8.0 * (first_head + 1.0 + head_index) / all_heads)


def attend(query, key_prefix, value_prefix, key_turn, value_turn, prefix_count, turn_count, slopes):
    turn_span = query.shape[0]
    prefix_span = key_prefix.shape[0]
    scale = query.shape[-1] ** -0.5
    query_wide = query.astype(jnp.float32)
    scores_prefix = jnp.einsum("ihd,phd->hip", query_wide, key_prefix.astype(jnp.float32)) * scale
    scores_turn = jnp.einsum("ihd,jhd->hij", query_wide, key_turn.astype(jnp.float32)) * scale
    rows = jnp.arange(turn_span, dtype=jnp.int32)
    columns = jnp.arange(prefix_span, dtype=jnp.int32)
    distance_prefix = (prefix_count + rows[:, None] - columns[None, :]).astype(jnp.float32)
    distance_turn = (rows[:, None] - rows[None, :]).astype(jnp.float32)
    scores_prefix = scores_prefix - slopes[:, None, None] * distance_prefix[None]
    scores_turn = scores_turn - slopes[:, None, None] * distance_turn[None]
    live_prefix = (columns < prefix_count)[None, None, :]
    live_turn = ((rows[None, :] <= rows[:, None]) & (rows[None, :] < turn_count))[None]
    scores = jnp.concatenate([jnp.where(live_prefix, scores_prefix, -jnp.inf), jnp.where(live_turn, scores_turn, -jnp.inf)], axis=-1)
    top = jnp.max(scores, axis=-1, keepdims=True)
    expo = jnp.exp(scores - top)
    weights = (expo / jnp.sum(expo, axis=-1, keepdims=True)).astype(jnp.bfloat16)
    values = jnp.concatenate([value_prefix, value_turn], axis=0).astype(jnp.float32)
    context = jnp.einsum("hik,khd->ihd", weights.astype(jnp.float32), values)
    return context.astype(jnp.bfloat16)


def reference(prefix_store, page_owner, prefix_len, turn_rows, turn_len, w_query, w_key, w_value):
    slopes = alibi_slopes(jnp.arange(HEADS).astype(jnp.float32))

    def project(rows, weight):
        result = jnp.dot(rows, weight, preferred_element_type=jnp.float32).astype(jnp.bfloat16)
        return result.reshape(rows.shape[0], HEADS, HS)

    def attend_one(items):
        owner_row, prefix_count, turn_part, turn_count = items
        fetched = jnp.take(prefix_store, owner_row.astype(jnp.int32), axis=0).reshape(PREFIX, D)
        key_prefix = project(fetched, w_key)
        value_prefix = project(fetched, w_value)
        query = project(turn_part, w_query)
        key_turn = project(turn_part, w_key)
        value_turn = project(turn_part, w_value)
        context = attend(query, key_prefix, value_prefix, key_turn, value_turn, prefix_count, turn_count, slopes)
        return context.reshape(TURN, HEADS * HS)

    return lax.map(attend_one, (page_owner, prefix_len, turn_rows, turn_len))
```

```python
import functools

import jax
import jax.numpy as jnp
from jax import lax
from jax.experimental import pallas as pl
from jax.experimental.pallas import tpu as pltpu
from jax.sharding import PartitionSpec as P

MESH = pl.DeviceIdType.MESH

SIDE = 4
TP = SIDE * SIDE
GROUPS = 8
HS = 128
HEADS_HERE = 4
COLS = HEADS_HERE * HS
WIDTH = 7168
SLICE = WIDTH // TP
PAGE = 128
PAGES = 4
CONVS = 2
TURN = 256
PREFIX = 512
HALF = PAGE // 2
BLOCK = 7 * HALF
PART = BLOCK // 2
TURN_CHUNKS = CONVS * TURN // PAGE
CHUNKS = TURN_CHUNKS + CONVS * PAGES
WIDE = 256
FIRST_HEAD = 48.0
ALL_HEADS = 112.0
BF = jnp.bfloat16
F32 = jnp.float32


def pack(rows, odd):
    wide = rows.astype(F32)
    main = jnp.where(odd, wide[:, 64:], wide[:, : 3 * 128])
    loose = jnp.where(odd, wide[:, :64], wide[:, 3 * 128 :])
    low = jnp.where(odd, loose[HALF:], loose[:HALF])
    high = jnp.where(odd, loose[:HALF], loose[HALF:])
    pieces = [
        main[h * HALF : (h + 1) * HALF, j * 128 : (j + 1) * 128]
        for j in range(3)
        for h in range(2)
    ]
    pieces.append(jnp.concatenate([low, high], axis=1))
    return jnp.concatenate(pieces, axis=0).astype(BF)


def kernel(
    owner_ref,
    prefix_len_ref,
    turn_len_ref,
    store_ref,
    turn_ref,
    wq_ref,
    wk_ref,
    wv_ref,
    out_ref,
    held,
    pages_out,
    pages_in,
    weight,
    whole,
    from_turn,
    from_prefix,
    weight_sem,
    page_send,
    page_recv,
    send_sem,
    recv_sem,
):
    group = lax.axis_index("group")
    tp = lax.axis_index("tp")
    y, z = tp // SIDE, tp % SIDE
    odd = tp % 2 == 1

    neighbour = [
        [((y + 1) % SIDE) * SIDE + z, ((y + SIDE - 1) % SIDE) * SIDE + z],
        [y * SIDE + (z + 1) % SIDE, y * SIDE + (z + SIDE - 1) % SIDE],
    ]

    barrier = pltpu.get_barrier_semaphore()
    for axis in range(2):
        for way in range(2):
            pl.semaphore_signal(
                barrier, inc=1, device_id=(group, neighbour[axis][way]), device_id_type=MESH
            )
    for off in range(1, GROUPS):
        pl.semaphore_signal(
            barrier, inc=1, device_id=((group + off) % GROUPS, tp), device_id_type=MESH
        )

    loads = [
        pltpu.make_async_copy(source, weight.at[:, pl.ds(i * COLS, COLS)], weight_sem.at[i])
        for i, source in enumerate((wq_ref, wk_ref, wv_ref))
    ]
    for load in loads:
        load.start()

    for chunk in range(TURN_CHUNKS):
        rows = turn_ref[chunk // 2, pl.ds((chunk % 2) * PAGE, PAGE), :]
        held[chunk, 0] = pack(rows, odd)

    pl.semaphore_wait(barrier, 4 + GROUPS - 1)

    def copy(chunk, source, target, axis, way, half):
        part = pl.ds(0, BLOCK) if half is None else pl.ds(half * PART, PART)
        sem = 0 if half is None else half
        return pltpu.make_async_remote_copy(
            src_ref=held.at[chunk, source, part],
            dst_ref=held.at[chunk, target, part],
            send_sem=send_sem.at[chunk, target, sem],
            recv_sem=recv_sem.at[chunk, target, sem],
            device_id=(group, neighbour[axis][way]),
            device_id_type=MESH,
        )

    def chunks_of(pair):
        return [(2 * pair, 0), (2 * pair + 1, 1)]

    def near_first(pair):
        return [
            copy(chunk, 0, (3 - 2 * way) * SIDE, axis, way, None)
            for chunk, axis in chunks_of(pair)
            for way in range(2)
        ]

    def far_first(pair):
        return [
            copy(chunk, (3 - 2 * way) * SIDE, 2 * SIDE, axis, way, way)
            for chunk, axis in chunks_of(pair)
            for way in range(2)
        ]

    def near_second(pair, which):
        return [
            copy(chunk, i * SIDE, i * SIDE + 3 - 2 * way, 1 - axis, way, None)
            for i in which
            for chunk, axis in chunks_of(pair)
            for way in range(2)
        ]

    def far_second(pair, which):
        return [
            copy(chunk, i * SIDE + 3 - 2 * way, i * SIDE + 2, 1 - axis, way, way)
            for i in which
            for chunk, axis in chunks_of(pair)
            for way in range(2)
        ]

    def start(copies):
        for one in copies:
            one.start()

    def arrived(copies):
        for one in copies:
            one.wait_recv()

    def left(copies):
        for one in copies:
            one.wait_send()

    def stage_a(pairs):
        for pair in pairs:
            start(near_first(pair))
        for pair in pairs:
            start(near_second(pair, (0,)))

    def stage_b(pairs):
        for pair in pairs:
            arrived(near_first(pair))
            start(far_first(pair))
            start(near_second(pair, (1, 3)))

    def stage_c(pairs):
        for pair in pairs:
            arrived(far_first(pair))
            start(near_second(pair, (2,)))
            arrived(near_second(pair, (0,)))
            start(far_second(pair, (0,)))

    def stage_d(pairs):
        for pair in pairs:
            arrived(near_second(pair, (1, 3)))
            start(far_second(pair, (1, 3)))
        for pair in pairs:
            arrived(near_second(pair, (2,)))
            start(far_second(pair, (2,)))

    def gathered(pair):
        arrived(far_second(pair, (0, 1, 2, 3)))

    def all_left(pair):
        left(near_first(pair))
        left(far_first(pair))
        left(near_second(pair, (0, 1, 2, 3)))

    def owner(page):
        return owner_ref[page // PAGES, page % PAGES]

    def stage_pages(to, carry):
        found = jnp.int32(0)
        first = jnp.int32(0)
        second = jnp.int32(0)
        for j in range(CONVS * PAGES):
            slot = owner(to * (CONVS * PAGES) + j)
            mine = slot // GROUPS == group
            first = jnp.where(mine & (found == 0), slot % GROUPS, first)
            second = jnp.where(mine & (found == 1), slot % GROUPS, second)
            found = found + mine.astype(jnp.int32)
        pages_out[to, 0] = store_ref[first]
        pages_out[to, 1] = store_ref[second]
        return carry

    def exchange(off, at):
        return pltpu.make_async_remote_copy(
            src_ref=pages_out.at[(group + off) % GROUPS],
            dst_ref=pages_in.at[at],
            send_sem=page_send.at[off],
            recv_sem=page_recv.at[off],
            device_id=((group + off) % GROUPS, tp),
            device_id_type=MESH,
        )

    def take_page(i, carry):
        source = owner(group * (CONVS * PAGES) + i) // GROUPS
        earlier = jnp.int32(0)
        for j in range(CONVS * PAGES):
            same = owner(group * (CONVS * PAGES) + j) // GROUPS == source
            earlier = earlier + (same & (j < i)).astype(jnp.int32)
        held[TURN_CHUNKS + i, 0] = pack(pages_in[source, jnp.minimum(earlier, 1)], odd)
        return carry

    lane = lax.broadcasted_iota(jnp.int32, (HALF, 128), 1)

    def lay_out(pair):
        def two(v, carry):
            def slot_of(device, axis):
                on_y = (device // SIDE - y + SIDE) % SIDE
                on_z = (device % SIDE - z + SIDE) % SIDE
                return on_y * SIDE + on_z if axis == 0 else on_z * SIDE + on_y

            base = v * (2 * SLICE)
            for chunk, axis in chunks_of(pair):
                even_at, odd_at = slot_of(2 * v, axis), slot_of(2 * v + 1, axis)

                def piece(slot, i):
                    return held[chunk, slot, pl.ds(i * HALF, HALF), :]

                top = pl.ds(axis * PAGE, HALF)
                low = pl.ds(axis * PAGE + HALF, HALF)
                for j in range(3):
                    for h, rows in enumerate((top, low)):
                        at = pl.multiple_of(base + j * 128, 128)
                        whole[rows, pl.ds(at, 128)] = piece(even_at, 2 * j + h)
                        at = pl.multiple_of(base + (4 + j) * 128, 128)
                        whole[rows, pl.ds(at, 128)] = piece(odd_at, 2 * j + h)
                evens, odds = piece(even_at, 6).astype(F32), piece(odd_at, 6).astype(F32)
                at = pl.multiple_of(base + 3 * 128, 128)
                whole[top, pl.ds(at, 128)] = jnp.where(lane < HALF, evens, odds).astype(BF)
                mixed = pltpu.roll(jnp.where(lane < HALF, odds, evens), HALF, axis=1)
                whole[low, pl.ds(at, 128)] = mixed.astype(BF)
            return carry

        lax.fori_loop(0, TP // 2, two, 0)

    def project(pair):
        lay_out(pair)

        def turn_columns(n, carry):
            at = pl.ds(pl.multiple_of(n * WIDE, WIDE), WIDE)
            term = jnp.dot(whole[...], weight[:, at], preferred_element_type=F32)
            from_turn[pair, :, at] = term.astype(BF)
            return carry

        def prefix_columns(n, carry):
            at = pl.ds(pl.multiple_of(n * WIDE, WIDE), WIDE)
            of = pl.ds(pl.multiple_of(COLS + n * WIDE, WIDE), WIDE)
            term = jnp.dot(whole[...], weight[:, of], preferred_element_type=F32)
            conv, half = (pair - CONVS) // 2, (pair - CONVS) % 2
            from_prefix[conv, pl.ds(half * WIDE, WIDE), at] = term.astype(BF)
            return carry

        if pair < CONVS:
            lax.fori_loop(0, 3 * COLS // WIDE, turn_columns, 0)
        else:
            lax.fori_loop(0, 2 * COLS // WIDE, prefix_columns, 0)

    def attend(conv, head):
        number = (tp * HEADS_HERE + head).astype(F32)
        power = jnp.full((1, 128), 1.0, F32) * (-8.0 * (FIRST_HEAD + 1.0 + number) / ALL_HEADS)
        slope = jnp.exp2(power)[:, :1]

        def columns(which):
            return pl.ds(pl.multiple_of(which * COLS + head * HS, HS), HS)

        def dots(left_side, right_side):
            return lax.dot_general(
                left_side, right_side, (((1,), (1,)), ((), ())), preferred_element_type=F32
            ) * (HS**-0.5)

        query = from_turn[conv, :, columns(0)]
        on_prefix = dots(query, from_prefix[conv, :, columns(0)])
        on_turn = dots(query, from_turn[conv, :, columns(1)])
        prefix_count, turn_count = prefix_len_ref[conv], turn_len_ref[conv]
        i = lax.broadcasted_iota(jnp.int32, (TURN, PREFIX), 0)
        j = lax.broadcasted_iota(jnp.int32, (TURN, PREFIX), 1)
        away = (prefix_count + i - j).astype(F32)
        on_prefix = jnp.where(j < prefix_count, on_prefix - slope * away, -jnp.inf)
        i = lax.broadcasted_iota(jnp.int32, (TURN, TURN), 0)
        j = lax.broadcasted_iota(jnp.int32, (TURN, TURN), 1)
        away = (i - j).astype(F32)
        live = j < jnp.minimum(i + 1, turn_count)
        on_turn = jnp.where(live, on_turn - slope * away, -jnp.inf)
        top = jnp.maximum(
            jnp.max(on_prefix, axis=1, keepdims=True), jnp.max(on_turn, axis=1, keepdims=True)
        )
        on_prefix, on_turn = jnp.exp(on_prefix - top), jnp.exp(on_turn - top)
        share = 1.0 / (
            jnp.sum(on_prefix, axis=1, keepdims=True) + jnp.sum(on_turn, axis=1, keepdims=True)
        )
        context = jnp.dot(
            (on_prefix * share).astype(BF),
            from_prefix[conv, :, columns(1)],
            preferred_element_type=F32,
        ) + jnp.dot(
            (on_turn * share).astype(BF), from_turn[conv, :, columns(2)], preferred_element_type=F32
        )
        out_ref[conv, :, columns(0)] = context.astype(BF)

    def attend_some(conv, lo, hi):
        def one(head, carry):
            attend(conv, head)
            return carry

        lax.fori_loop(lo, hi, one, 0)

    stage_a((0, 1))
    lax.fori_loop(0, GROUPS, stage_pages, 0)
    for off in range(1, GROUPS):
        exchange(off, group).start()
    pages_in[group] = pages_out[group]
    stage_b((0, 1))
    stage_c((0, 1))
    for off in range(1, GROUPS):
        exchange(off, (group - off + GROUPS) % GROUPS).wait()
    lax.fori_loop(0, PAGES, take_page, 0)
    stage_a((2, 3))
    stage_d((0, 1))
    lax.fori_loop(PAGES, 2 * PAGES, take_page, 0)
    stage_b((2, 3))
    for load in loads:
        load.wait()
    gathered(0)
    project(0)
    stage_c((2, 3))
    stage_a((4, 5))
    gathered(1)
    project(1)
    stage_d((2, 3))
    stage_b((4, 5))
    for pair in (0, 1):
        all_left(pair)
        left(far_second(pair, (0, 1, 2, 3)))
    gathered(2)
    project(2)
    stage_c((4, 5))
    gathered(3)
    project(3)
    stage_d((4, 5))
    attend_some(0, 0, HEADS_HERE)
    for pair in (2, 3):
        all_left(pair)
        left(far_second(pair, (0, 1, 2, 3)))
    for pair in (4, 5):
        all_left(pair)
    gathered(4)
    project(4)
    gathered(5)
    project(5)
    for pair in (4, 5):
        left(far_second(pair, (0, 1, 2, 3)))
    attend_some(1, 0, HEADS_HERE)


def body(prefix_store, page_owner, prefix_len, turn_rows, turn_len, w_query, w_key, w_value):
    vmem = pl.BlockSpec(memory_space=pltpu.VMEM)
    smem = pl.BlockSpec(memory_space=pltpu.SMEM)
    hbm = pl.BlockSpec(memory_space=pl.ANY)
    return pl.pallas_call(
        kernel,
        out_shape=jax.ShapeDtypeStruct((CONVS, TURN, COLS), BF),
        in_specs=[smem, smem, smem, vmem, vmem, hbm, hbm, hbm],
        out_specs=vmem,
        scratch_shapes=[
            pltpu.VMEM((CHUNKS, TP, BLOCK, 128), BF),
            pltpu.VMEM((GROUPS, 2, PAGE, SLICE), BF),
            pltpu.VMEM((GROUPS, 2, PAGE, SLICE), BF),
            pltpu.VMEM((WIDTH, 3 * COLS), BF),
            pltpu.VMEM((2 * PAGE, WIDTH), BF),
            pltpu.VMEM((CONVS, TURN, 3 * COLS), BF),
            pltpu.VMEM((CONVS, PREFIX, 2 * COLS), BF),
            pltpu.SemaphoreType.DMA((3,)),
            pltpu.SemaphoreType.DMA((GROUPS,)),
            pltpu.SemaphoreType.DMA((GROUPS,)),
            pltpu.SemaphoreType.DMA((CHUNKS, TP, 2)),
            pltpu.SemaphoreType.DMA((CHUNKS, TP, 2)),
        ],
        compiler_params=pltpu.CompilerParams(
            collective_id=0, has_side_effects=True, vmem_limit_bytes=63 * 2**20
        ),
        cost_estimate=pl.CostEstimate(
            flops=27_000_000_000, bytes_accessed=26_000_000, transcendentals=1_600_000
        ),
        name="resume_attention",
    )(page_owner, prefix_len, turn_len, prefix_store, turn_rows, w_query, w_key, w_value)


def solution(mesh):
    in_specs = (
        P("group", None, "tp"),
        P(),
        P("group"),
        P("group", None, "tp"),
        P("group"),
        P(None, "tp"),
        P(None, "tp"),
        P(None, "tp"),
    )
    out_specs = P("group", None, "tp")
    return jax.shard_map(body, mesh=mesh, in_specs=in_specs, out_specs=out_specs, check_vma=False)
```

```python
import functools

import jax
import jax.numpy as jnp
from jax import lax
from jax.experimental import pallas as pl
from jax.experimental.pallas import tpu as pltpu
from jax.sharding import PartitionSpec as P

MESH = pl.DeviceIdType.MESH

SIDE = 4
TP = SIDE * SIDE
GROUPS = 8
HS = 128
HEADS_HERE = 4
COLS = HEADS_HERE * HS
WIDTH = 7168
SLICE = WIDTH // TP
PAGE = 128
PAGES = 4
CONVS = 2
TURN = 256
PREFIX = 512
PART = SLICE // 2
TURN_CHUNKS = CONVS * TURN // PAGE
CHUNKS = TURN_CHUNKS + CONVS * PAGES
WIDE = 256
FIRST_HEAD = 48.0
ALL_HEADS = 112.0
BF = jnp.bfloat16
F32 = jnp.float32


def kernel(
    owner_ref,
    prefix_len_ref,
    turn_len_ref,
    store_hbm,
    turn_hbm,
    wq_ref,
    wk_ref,
    wv_ref,
    out_hbm,
    store_ref,
    out_ref,
    part_top,
    part_sum,
    part_context,
    held,
    pages_out,
    pages_in,
    weight,
    whole,
    from_turn,
    from_prefix,
    own_sem,
    out_sem,
    weight_sem,
    page_send,
    page_recv,
    send_sem,
    recv_sem,
):
    group = lax.axis_index("group")
    tp = lax.axis_index("tp")
    y, z = tp // SIDE, tp % SIDE

    neighbour = [
        [((y + 1) % SIDE) * SIDE + z, ((y + SIDE - 1) % SIDE) * SIDE + z],
        [y * SIDE + (z + 1) % SIDE, y * SIDE + (z + SIDE - 1) % SIDE],
    ]

    fetch_turn = [
        pltpu.make_async_copy(
            turn_hbm.at[chunk // 2, :, pl.ds((chunk % 2) * PAGE, PAGE)],
            held.at[chunk, 0],
            own_sem.at[chunk],
        )
        for chunk in range(TURN_CHUNKS)
    ]
    fetch_store = pltpu.make_async_copy(store_hbm, store_ref, own_sem.at[TURN_CHUNKS])
    for fetch in fetch_turn:
        fetch.start()
    fetch_store.start()

    barrier = pltpu.get_barrier_semaphore()
    for axis in range(2):
        for way in range(2):
            pl.semaphore_signal(
                barrier, inc=1, device_id=(group, neighbour[axis][way]), device_id_type=MESH
            )
    for off in range(1, GROUPS):
        pl.semaphore_signal(
            barrier, inc=1, device_id=((group + off) % GROUPS, tp), device_id_type=MESH
        )

    loads = [
        pltpu.make_async_copy(source, weight.at[:, pl.ds(i * COLS, COLS)], weight_sem.at[i])
        for i, source in enumerate((wq_ref, wk_ref, wv_ref))
    ]
    for fetch in fetch_turn:
        fetch.wait()
    pl.semaphore_wait(barrier, 4 + GROUPS - 1)

    def copy(chunk, source, target, axis, way, half):
        part = pl.ds(0, SLICE) if half is None else pl.ds(half * PART, PART)
        sem = 0 if half is None else half
        return pltpu.make_async_remote_copy(
            src_ref=held.at[chunk, source, part],
            dst_ref=held.at[chunk, target, part],
            send_sem=send_sem.at[chunk, target, sem],
            recv_sem=recv_sem.at[chunk, target, sem],
            device_id=(group, neighbour[axis][way]),
            device_id_type=MESH,
        )

    def chunks_of(pair):
        return [(2 * pair, 0), (2 * pair + 1, 1)]

    def near_first(pair):
        return [
            copy(chunk, 0, (3 - 2 * way) * SIDE, axis, way, None)
            for chunk, axis in chunks_of(pair)
            for way in range(2)
        ]

    def far_first(pair):
        return [
            copy(chunk, (3 - 2 * way) * SIDE, 2 * SIDE, axis, way, way)
            for chunk, axis in chunks_of(pair)
            for way in range(2)
        ]

    def near_second(pair, which):
        return [
            copy(chunk, i * SIDE, i * SIDE + 3 - 2 * way, 1 - axis, way, None)
            for i in which
            for chunk, axis in chunks_of(pair)
            for way in range(2)
        ]

    def far_second(pair, which):
        return [
            copy(chunk, i * SIDE + 3 - 2 * way, i * SIDE + 2, 1 - axis, way, way)
            for i in which
            for chunk, axis in chunks_of(pair)
            for way in range(2)
        ]

    def start(copies):
        for one in copies:
            one.start()

    def arrived(copies):
        for one in copies:
            one.wait_recv()

    def left(copies):
        for one in copies:
            one.wait_send()

    def stage_a(pairs):
        for pair in pairs:
            start(near_first(pair))
        for pair in pairs:
            start(near_second(pair, (0,)))

    def stage_b(pairs):
        for pair in pairs:
            arrived(near_first(pair))
            start(far_first(pair))
            start(near_second(pair, (1, 3)))

    def stage_c(pairs):
        for pair in pairs:
            arrived(far_first(pair))
            start(near_second(pair, (2,)))
            arrived(near_second(pair, (0,)))
            start(far_second(pair, (0,)))

    def stage_d(pairs):
        for pair in pairs:
            arrived(near_second(pair, (1, 3)))
            start(far_second(pair, (1, 3)))
        for pair in pairs:
            arrived(near_second(pair, (2,)))
            start(far_second(pair, (2,)))

    def gathered(pair):
        arrived(far_second(pair, (0, 1, 2, 3)))

    def all_left(pair):
        left(near_first(pair))
        left(far_first(pair))
        left(near_second(pair, (0, 1, 2, 3)))

    def owner(page):
        return owner_ref[page % PAGES, page // PAGES]

    def stage_pages(to, carry):
        found = jnp.int32(0)
        first = jnp.int32(0)
        second = jnp.int32(0)
        for j in range(CONVS * PAGES):
            slot = owner(to * (CONVS * PAGES) + j)
            mine = slot // GROUPS == group
            first = jnp.where(mine & (found == 0), slot % GROUPS, first)
            second = jnp.where(mine & (found == 1), slot % GROUPS, second)
            found = found + mine.astype(jnp.int32)
        pages_out[to, 0] = store_ref[first]
        pages_out[to, 1] = store_ref[second]
        return carry

    def exchange(off, at):
        return pltpu.make_async_remote_copy(
            src_ref=pages_out.at[(group + off) % GROUPS],
            dst_ref=pages_in.at[at],
            send_sem=page_send.at[off],
            recv_sem=page_recv.at[off],
            device_id=((group + off) % GROUPS, tp),
            device_id_type=MESH,
        )

    def take_page(i, carry):
        source = owner(group * (CONVS * PAGES) + i) // GROUPS
        earlier = jnp.int32(0)
        for j in range(CONVS * PAGES):
            same = owner(group * (CONVS * PAGES) + j) // GROUPS == source
            earlier = earlier + (same & (j < i)).astype(jnp.int32)
        held[TURN_CHUNKS + i, 0] = pages_in[source, jnp.minimum(earlier, 1)]
        return carry

    def lay_out(pair):
        def two(v, carry):
            def slot_of(device, axis):
                on_y = (device // SIDE - y + SIDE) % SIDE
                on_z = (device % SIDE - z + SIDE) % SIDE
                return on_y * SIDE + on_z if axis == 0 else on_z * SIDE + on_y

            at = pl.ds(pl.multiple_of(v * (2 * SLICE), 128), 2 * SLICE)
            for chunk, axis in chunks_of(pair):
                blocks = [held[chunk, slot_of(2 * v + k, axis)] for k in range(2)]
                whole[pl.ds(axis * PAGE, PAGE), at] = jnp.concatenate(blocks, axis=0).T
            return carry

        lax.fori_loop(0, TP // 2, two, 0)

    def project(pair):
        lay_out(pair)

        def turn_columns(n, carry):
            at = pl.ds(pl.multiple_of(n * WIDE, WIDE), WIDE)
            term = jnp.dot(whole[...], weight[:, at], preferred_element_type=F32)
            from_turn[pair, :, at] = term.astype(BF)
            return carry

        def prefix_columns(n, carry):
            at = pl.ds(pl.multiple_of(n * WIDE, WIDE), WIDE)
            of = pl.ds(pl.multiple_of(COLS + n * WIDE, WIDE), WIDE)
            term = jnp.dot(whole[...], weight[:, of], preferred_element_type=F32)
            conv, half = (pair - CONVS) // 2, (pair - CONVS) % 2
            from_prefix[conv, pl.ds(half * WIDE, WIDE), at] = term.astype(BF)
            return carry

        if pair < CONVS:
            lax.fori_loop(0, 3 * COLS // WIDE, turn_columns, 0)
        else:
            lax.fori_loop(0, 2 * COLS // WIDE, prefix_columns, 0)

    def slope_of(head):
        number = (tp * HEADS_HERE + head).astype(F32)
        power = jnp.full((1, 128), 1.0, F32) * (-8.0 * (FIRST_HEAD + 1.0 + number) / ALL_HEADS)
        return jnp.exp2(power)[:, :1]

    def columns(which, head):
        return pl.ds(pl.multiple_of(which * COLS + head * HS, HS), HS)

    def dots(left_side, right_side):
        return lax.dot_general(
            left_side, right_side, (((1,), (1,)), ((), ())), preferred_element_type=F32
        ) * (HS**-0.5)

    def prefix_scores(conv, head, lo, count):
        scores = dots(
            from_turn[conv, :, columns(0, head)], from_prefix[conv, pl.ds(lo, count), columns(0, head)]
        )
        i = lax.broadcasted_iota(jnp.int32, (TURN, count), 0)
        j = lax.broadcasted_iota(jnp.int32, (TURN, count), 1) + lo
        away = (prefix_len_ref[conv] + i - j).astype(F32)
        return jnp.where(j < prefix_len_ref[conv], scores - slope_of(head) * away, -jnp.inf)

    def turn_scores(conv, head):
        scores = dots(from_turn[conv, :, columns(0, head)], from_turn[conv, :, columns(1, head)])
        i = lax.broadcasted_iota(jnp.int32, (TURN, TURN), 0)
        j = lax.broadcasted_iota(jnp.int32, (TURN, TURN), 1)
        away = (i - j).astype(F32)
        live = j < jnp.minimum(i + 1, turn_len_ref[conv])
        return jnp.where(live, scores - slope_of(head) * away, -jnp.inf)

    def highest(scores):
        return jnp.max(scores, axis=1, keepdims=True)

    def summed(scores):
        return jnp.sum(scores, axis=1, keepdims=True)

    def prefix_values(conv, head, lo, count, weights):
        return jnp.dot(
            weights.astype(BF),
            from_prefix[conv, pl.ds(lo, count), columns(1, head)],
            preferred_element_type=F32,
        )

    def turn_values(conv, head, weights):
        return jnp.dot(
            weights.astype(BF), from_turn[conv, :, columns(2, head)], preferred_element_type=F32
        )

    def attend(conv, head):
        on_prefix, on_turn = prefix_scores(conv, head, 0, PREFIX), turn_scores(conv, head)
        top = jnp.maximum(highest(on_prefix), highest(on_turn))
        on_prefix, on_turn = jnp.exp(on_prefix - top), jnp.exp(on_turn - top)
        share = 1.0 / (summed(on_prefix) + summed(on_turn))
        context = prefix_values(conv, head, 0, PREFIX, on_prefix * share)
        context = context + turn_values(conv, head, on_turn * share)
        out_ref[conv, :, columns(0, head)] = context.astype(BF)

    def attend_early(conv, head):
        on_prefix, on_turn = prefix_scores(conv, head, 0, PREFIX // 2), turn_scores(conv, head)
        top = jnp.maximum(highest(on_prefix), highest(on_turn))
        on_prefix, on_turn = jnp.exp(on_prefix - top), jnp.exp(on_turn - top)
        part_top[head] = jnp.broadcast_to(top, (TURN, 128))
        part_sum[head] = jnp.broadcast_to(summed(on_prefix) + summed(on_turn), (TURN, 128))
        part_context[head] = prefix_values(conv, head, 0, PREFIX // 2, on_prefix) + turn_values(
            conv, head, on_turn
        )

    def attend_late(conv, head):
        on_prefix = prefix_scores(conv, head, PREFIX // 2, PREFIX // 2)
        early_top = part_top[head, :, :1]
        top = jnp.maximum(early_top, highest(on_prefix))
        on_prefix = jnp.exp(on_prefix - top)
        kept = jnp.exp(early_top - top)
        total = part_sum[head, :, :1] * kept + summed(on_prefix)
        context = part_context[head] * kept + prefix_values(
            conv, head, PREFIX // 2, PREFIX // 2, on_prefix
        )
        out_ref[conv, :, columns(0, head)] = (context * (1.0 / total)).astype(BF)

    def some_heads(attention, conv, lo, hi):
        def one(head, carry):
            attention(conv, head)
            return carry

        lax.fori_loop(lo, hi, one, 0)

    def give(conv):
        return pltpu.make_async_copy(out_ref.at[conv], out_hbm.at[conv], out_sem.at[conv])

    stage_a((0, 1))
    fetch_store.wait()
    lax.fori_loop(0, GROUPS, stage_pages, 0)
    for off in range(1, GROUPS):
        exchange(off, group).start()
    for load in loads:
        load.start()
    pages_in[group] = pages_out[group]
    stage_b((0, 1))
    stage_c((0, 1))
    for off in range(1, GROUPS):
        exchange(off, (group - off + GROUPS) % GROUPS).wait()
    lax.fori_loop(0, PAGES, take_page, 0)
    stage_a((2, 3))
    stage_d((0, 1))
    lax.fori_loop(PAGES, 2 * PAGES, take_page, 0)
    stage_b((2, 3))
    for load in loads:
        load.wait()
    gathered(0)
    project(0)
    stage_c((2, 3))
    stage_a((4,))
    gathered(1)
    project(1)
    stage_d((2, 3))
    stage_b((4,))
    for pair in (0, 1):
        all_left(pair)
        left(far_second(pair, (0, 1, 2, 3)))
    gathered(2)
    project(2)
    stage_c((4,))
    stage_a((5,))
    gathered(3)
    project(3)
    stage_d((4,))
    stage_b((5,))
    some_heads(attend, 0, 0, 2)
    stage_c((5,))
    gathered(4)
    project(4)
    stage_d((5,))
    some_heads(attend, 0, 2, HEADS_HERE)
    give(0).start()
    some_heads(attend_early, 1, 0, HEADS_HERE)
    for pair in (2, 3, 4):
        all_left(pair)
        left(far_second(pair, (0, 1, 2, 3)))
    all_left(5)
    gathered(5)
    project(5)
    some_heads(attend_late, 1, 0, HEADS_HERE)
    give(1).start()
    left(far_second(5, (0, 1, 2, 3)))
    give(0).wait()
    give(1).wait()


def body(prefix_store, page_owner, prefix_len, turn_rows, turn_len, w_query, w_key, w_value):
    smem = pl.BlockSpec(memory_space=pltpu.SMEM)
    hbm = pl.BlockSpec(memory_space=pl.ANY)
    return pl.pallas_call(
        kernel,
        out_shape=jax.ShapeDtypeStruct((CONVS, TURN, COLS), BF),
        in_specs=[smem, smem, smem, hbm, hbm, hbm, hbm, hbm],
        out_specs=hbm,
        scratch_shapes=[
            pltpu.VMEM((GROUPS, SLICE, PAGE), BF),
            pltpu.VMEM((CONVS, TURN, COLS), BF),
            pltpu.VMEM((HEADS_HERE, TURN, 128), F32),
            pltpu.VMEM((HEADS_HERE, TURN, 128), F32),
            pltpu.VMEM((HEADS_HERE, TURN, HS), F32),
            pltpu.VMEM((CHUNKS, TP, SLICE, 128), BF),
            pltpu.VMEM((GROUPS, 2, SLICE, PAGE), BF),
            pltpu.VMEM((GROUPS, 2, SLICE, PAGE), BF),
            pltpu.VMEM((WIDTH, 3 * COLS), BF),
            pltpu.VMEM((2 * PAGE, WIDTH), BF),
            pltpu.VMEM((CONVS, TURN, 3 * COLS), BF),
            pltpu.VMEM((CONVS, PREFIX, 2 * COLS), BF),
            pltpu.SemaphoreType.DMA((TURN_CHUNKS + 1,)),
            pltpu.SemaphoreType.DMA((CONVS,)),
            pltpu.SemaphoreType.DMA((3,)),
            pltpu.SemaphoreType.DMA((GROUPS,)),
            pltpu.SemaphoreType.DMA((GROUPS,)),
            pltpu.SemaphoreType.DMA((CHUNKS, TP, 2)),
            pltpu.SemaphoreType.DMA((CHUNKS, TP, 2)),
        ],
        compiler_params=pltpu.CompilerParams(
            collective_id=0, has_side_effects=True, vmem_limit_bytes=63 * 2**20
        ),
        cost_estimate=pl.CostEstimate(
            flops=27_000_000_000, bytes_accessed=26_000_000, transcendentals=1_600_000
        ),
        name="resume_attention",
    )(
        page_owner.T,
        prefix_len,
        turn_len,
        jnp.swapaxes(prefix_store, 1, 2),
        jnp.swapaxes(turn_rows, 1, 2),
        w_query,
        w_key,
        w_value,
    )


def solution(mesh):
    in_specs = (
        P("group", None, "tp"),
        P(),
        P("group"),
        P("group", None, "tp"),
        P("group"),
        P(None, "tp"),
        P(None, "tp"),
        P(None, "tp"),
    )
    out_specs = P("group", None, "tp")
    return jax.shard_map(body, mesh=mesh, in_specs=in_specs, out_specs=out_specs, check_vma=False)
```

```python
import functools

import jax
import jax.numpy as jnp
from jax import lax
from jax.experimental import pallas as pl
from jax.experimental.pallas import tpu as pltpu
from jax.sharding import PartitionSpec as P

MESH = pl.DeviceIdType.MESH

SIDE = 4
TP = SIDE * SIDE
GROUPS = 8
HS = 128
HEADS_HERE = 4
COLS = HEADS_HERE * HS
WIDTH = 7168
SLICE = WIDTH // TP
PAGE = 128
PAGES = 4
CONVS = 2
TURN = 256
PREFIX = 512
PART = SLICE // 2
SENT = 15
TURN_CHUNKS = CONVS * TURN // PAGE
CHUNKS = TURN_CHUNKS + CONVS * PAGES
WIDE = 256
FIRST_HEAD = 48.0
ALL_HEADS = 112.0
BF = jnp.bfloat16
F32 = jnp.float32


def kernel(
    owner_ref,
    prefix_len_ref,
    turn_len_ref,
    store_hbm,
    turn_hbm,
    wq_ref,
    wk_ref,
    wv_ref,
    out_hbm,
    store_ref,
    out_ref,
    part_top,
    part_sum,
    part_context,
    held,
    pages_out,
    pages_in,
    weight,
    whole,
    from_turn,
    from_prefix,
    own_sem,
    out_sem,
    weight_sem,
    page_send,
    page_recv,
    send_sem,
    recv_sem,
):
    group = lax.axis_index("group")
    tp = lax.axis_index("tp")
    y, z = tp // SIDE, tp % SIDE

    neighbour = [
        [((y + 1) % SIDE) * SIDE + z, ((y + SIDE - 1) % SIDE) * SIDE + z],
        [y * SIDE + (z + 1) % SIDE, y * SIDE + (z + SIDE - 1) % SIDE],
    ]

    fetch_turn = [
        pltpu.make_async_copy(
            turn_hbm.at[chunk // 2, :, pl.ds((chunk % 2) * PAGE, PAGE)],
            held.at[chunk, 0],
            own_sem.at[chunk],
        )
        for chunk in range(TURN_CHUNKS)
    ]
    fetch_store = pltpu.make_async_copy(store_hbm, store_ref, own_sem.at[TURN_CHUNKS])
    for fetch in fetch_turn:
        fetch.start()
    fetch_store.start()

    barrier = pltpu.get_barrier_semaphore()
    for axis in range(2):
        for way in range(2):
            pl.semaphore_signal(
                barrier, inc=1, device_id=(group, neighbour[axis][way]), device_id_type=MESH
            )
    for off in range(1, GROUPS):
        pl.semaphore_signal(
            barrier, inc=1, device_id=((group + off) % GROUPS, tp), device_id_type=MESH
        )

    loads = [
        pltpu.make_async_copy(source, weight.at[:, pl.ds(i * COLS, COLS)], weight_sem.at[i])
        for i, source in enumerate((wq_ref, wk_ref, wv_ref))
    ]
    for fetch in fetch_turn:
        fetch.wait()
    pl.semaphore_wait(barrier, 4 + GROUPS - 1)

    def copy(chunk, source, target, axis, way, half):
        part = pl.ds(0, SLICE) if half is None else pl.ds(half * PART, PART)
        sem = 0 if half is None else half
        return pltpu.make_async_remote_copy(
            src_ref=held.at[chunk, source, part],
            dst_ref=held.at[chunk, target, part],
            send_sem=send_sem.at[chunk],
            recv_sem=recv_sem.at[chunk, target, sem],
            device_id=(group, neighbour[axis][way]),
            device_id_type=MESH,
        )

    def chunks_of(pair):
        return [(2 * pair, 0), (2 * pair + 1, 1)]

    def near_first(pair):
        return [
            copy(chunk, 0, (3 - 2 * way) * SIDE, axis, way, None)
            for chunk, axis in chunks_of(pair)
            for way in range(2)
        ]

    def far_first(pair):
        return [
            copy(chunk, (3 - 2 * way) * SIDE, 2 * SIDE, axis, way, way)
            for chunk, axis in chunks_of(pair)
            for way in range(2)
        ]

    def near_second(pair, which):
        return [
            copy(chunk, i * SIDE, i * SIDE + 3 - 2 * way, 1 - axis, way, None)
            for i in which
            for chunk, axis in chunks_of(pair)
            for way in range(2)
        ]

    def far_second(pair, which):
        return [
            copy(chunk, i * SIDE + 3 - 2 * way, i * SIDE + 2, 1 - axis, way, way)
            for i in which
            for chunk, axis in chunks_of(pair)
            for way in range(2)
        ]

    def start(copies):
        for one in copies:
            one.start()

    def arrived(copies):
        for one in copies:
            one.wait_recv()

    def stage_a(pairs):
        for pair in pairs:
            start(near_first(pair))
        for pair in pairs:
            start(near_second(pair, (0,)))

    def stage_b(pairs):
        for pair in pairs:
            arrived(near_first(pair))
            start(far_first(pair))
            start(near_second(pair, (1, 3)))

    def stage_c(pairs):
        for pair in pairs:
            arrived(far_first(pair))
            start(near_second(pair, (2,)))
            arrived(near_second(pair, (0,)))
            start(far_second(pair, (0,)))

    def stage_d(pairs):
        for pair in pairs:
            arrived(near_second(pair, (1, 3)))
            start(far_second(pair, (1, 3)))
        for pair in pairs:
            arrived(near_second(pair, (2,)))
            start(far_second(pair, (2,)))

    def gathered(pair):
        arrived(far_second(pair, (0, 1, 2, 3)))

    def all_left(pair):
        for chunk, axis in chunks_of(pair):
            blocks = held.at[chunk, pl.ds(0, SENT)]
            pltpu.make_async_remote_copy(
                src_ref=blocks,
                dst_ref=blocks,
                send_sem=send_sem.at[chunk],
                recv_sem=recv_sem.at[chunk, 0, 0],
                device_id=(group, neighbour[axis][0]),
                device_id_type=MESH,
            ).wait_send()

    def owner(page):
        return owner_ref[page % PAGES, page // PAGES]

    def stage_pages(to, carry):
        found = jnp.int32(0)
        first = jnp.int32(0)
        second = jnp.int32(0)
        for j in range(CONVS * PAGES):
            slot = owner(to * (CONVS * PAGES) + j)
            mine = slot // GROUPS == group
            first = jnp.where(mine & (found == 0), slot % GROUPS, first)
            second = jnp.where(mine & (found == 1), slot % GROUPS, second)
            found = found + mine.astype(jnp.int32)
        pages_out[to, 0] = store_ref[first]
        pages_out[to, 1] = store_ref[second]
        return carry

    def exchange(off, at):
        return pltpu.make_async_remote_copy(
            src_ref=pages_out.at[(group + off) % GROUPS],
            dst_ref=pages_in.at[at],
            send_sem=page_send.at[off],
            recv_sem=page_recv.at[off],
            device_id=((group + off) % GROUPS, tp),
            device_id_type=MESH,
        )

    def take_page(i, carry):
        source = owner(group * (CONVS * PAGES) + i) // GROUPS
        earlier = jnp.int32(0)
        for j in range(CONVS * PAGES):
            same = owner(group * (CONVS * PAGES) + j) // GROUPS == source
            earlier = earlier + (same & (j < i)).astype(jnp.int32)
        held[TURN_CHUNKS + i, 0] = pages_in[source, jnp.minimum(earlier, 1)]
        return carry

    def lay_out(pair):
        def two(v, carry):
            def slot_of(device, axis):
                on_y = (device // SIDE - y + SIDE) % SIDE
                on_z = (device % SIDE - z + SIDE) % SIDE
                return on_y * SIDE + on_z if axis == 0 else on_z * SIDE + on_y

            at = pl.ds(pl.multiple_of(v * (2 * SLICE), 128), 2 * SLICE)
            for chunk, axis in chunks_of(pair):
                blocks = [held[chunk, slot_of(2 * v + k, axis)] for k in range(2)]
                whole[pl.ds(axis * PAGE, PAGE), at] = jnp.concatenate(blocks, axis=0).T
            return carry

        lax.fori_loop(0, TP // 2, two, 0)

    def project(pair):
        lay_out(pair)

        def turn_columns(n, carry):
            at = pl.ds(pl.multiple_of(n * WIDE, WIDE), WIDE)
            term = jnp.dot(whole[...], weight[:, at], preferred_element_type=F32)
            from_turn[pair, :, at] = term.astype(BF)
            return carry

        def prefix_columns(n, carry):
            at = pl.ds(pl.multiple_of(n * WIDE, WIDE), WIDE)
            of = pl.ds(pl.multiple_of(COLS + n * WIDE, WIDE), WIDE)
            term = jnp.dot(whole[...], weight[:, of], preferred_element_type=F32)
            conv, half = (pair - CONVS) // 2, (pair - CONVS) % 2
            from_prefix[conv, pl.ds(half * WIDE, WIDE), at] = term.astype(BF)
            return carry

        if pair < CONVS:
            lax.fori_loop(0, 3 * COLS // WIDE, turn_columns, 0)
        else:
            lax.fori_loop(0, 2 * COLS // WIDE, prefix_columns, 0)

    def last_columns(n):
        of = pl.ds(COLS + n * WIDE, WIDE)
        term = jnp.dot(whole[...], weight[:, of], preferred_element_type=F32)
        from_prefix[CONVS - 1, pl.ds(WIDE, WIDE), pl.ds(n * WIDE, WIDE)] = term.astype(BF)

    def slope_of(head):
        number = jnp.asarray(tp * HEADS_HERE + head, F32)
        power = jnp.full((1, 128), 1.0, F32) * (-8.0 * (FIRST_HEAD + 1.0 + number) / ALL_HEADS)
        return jnp.exp2(power)[:, :1]

    def columns(which, head):
        if isinstance(head, int):
            return pl.ds(which * COLS + head * HS, HS)
        return pl.ds(pl.multiple_of(which * COLS + head * HS, HS), HS)

    def dots(left_side, right_side):
        return lax.dot_general(
            left_side, right_side, (((1,), (1,)), ((), ())), preferred_element_type=F32
        ) * (HS**-0.5)

    def prefix_scores(conv, head, lo, count):
        scores = dots(
            from_turn[conv, :, columns(0, head)], from_prefix[conv, pl.ds(lo, count), columns(0, head)]
        )
        i = lax.broadcasted_iota(jnp.int32, (TURN, count), 0)
        j = lax.broadcasted_iota(jnp.int32, (TURN, count), 1) + lo
        away = (prefix_len_ref[conv] + i - j).astype(F32)
        return jnp.where(j < prefix_len_ref[conv], scores - slope_of(head) * away, -jnp.inf)

    def turn_scores(conv, head):
        scores = dots(from_turn[conv, :, columns(0, head)], from_turn[conv, :, columns(1, head)])
        i = lax.broadcasted_iota(jnp.int32, (TURN, TURN), 0)
        j = lax.broadcasted_iota(jnp.int32, (TURN, TURN), 1)
        away = (i - j).astype(F32)
        live = j < jnp.minimum(i + 1, turn_len_ref[conv])
        return jnp.where(live, scores - slope_of(head) * away, -jnp.inf)

    def highest(scores):
        return jnp.max(scores, axis=1, keepdims=True)

    def summed(scores):
        return jnp.sum(scores, axis=1, keepdims=True)

    def prefix_values(conv, head, lo, count, weights):
        return jnp.dot(
            weights.astype(BF),
            from_prefix[conv, pl.ds(lo, count), columns(1, head)],
            preferred_element_type=F32,
        )

    def turn_values(conv, head, weights):
        return jnp.dot(
            weights.astype(BF), from_turn[conv, :, columns(2, head)], preferred_element_type=F32
        )

    def attend(conv, head):
        on_prefix, on_turn = prefix_scores(conv, head, 0, PREFIX), turn_scores(conv, head)
        top = jnp.maximum(highest(on_prefix), highest(on_turn))
        on_prefix, on_turn = jnp.exp(on_prefix - top), jnp.exp(on_turn - top)
        share = 1.0 / (summed(on_prefix) + summed(on_turn))
        context = prefix_values(conv, head, 0, PREFIX, on_prefix * share)
        context = context + turn_values(conv, head, on_turn * share)
        out_ref[conv, :, columns(0, head)] = context.astype(BF)

    def attend_early(conv, head):
        on_prefix, on_turn = prefix_scores(conv, head, 0, PREFIX // 2), turn_scores(conv, head)
        top = jnp.maximum(highest(on_prefix), highest(on_turn))
        on_prefix, on_turn = jnp.exp(on_prefix - top), jnp.exp(on_turn - top)
        part_top[head] = jnp.broadcast_to(top, (TURN, 128))
        part_sum[head] = jnp.broadcast_to(summed(on_prefix) + summed(on_turn), (TURN, 128))
        part_context[head] = prefix_values(conv, head, 0, PREFIX // 2, on_prefix) + turn_values(
            conv, head, on_turn
        )

    def attend_late(conv, head):
        on_prefix = prefix_scores(conv, head, PREFIX // 2, PREFIX // 2)
        early_top = part_top[head, :, :1]
        top = jnp.maximum(early_top, highest(on_prefix))
        on_prefix = jnp.exp(on_prefix - top)
        kept = jnp.exp(early_top - top)
        total = part_sum[head, :, :1] * kept + summed(on_prefix)
        context = part_context[head] * kept + prefix_values(
            conv, head, PREFIX // 2, PREFIX // 2, on_prefix
        )
        out_ref[conv, :, columns(0, head)] = (context * (1.0 / total)).astype(BF)

    def some_heads(attention, conv, lo, hi):
        def one(head, carry):
            attention(conv, head)
            return carry

        lax.fori_loop(lo, hi, one, 0)

    def give(conv):
        return pltpu.make_async_copy(out_ref.at[conv], out_hbm.at[conv], out_sem.at[conv])

    stage_a((0, 1))
    fetch_store.wait()
    lax.fori_loop(0, GROUPS, stage_pages, 0)
    for off in range(1, GROUPS):
        exchange(off, group).start()
    for load in loads:
        load.start()
    pages_in[group] = pages_out[group]
    stage_b((0, 1))
    stage_c((0, 1))
    for off in range(1, GROUPS):
        exchange(off, (group - off + GROUPS) % GROUPS).wait()
    lax.fori_loop(0, PAGES, take_page, 0)
    stage_a((2, 3))
    stage_d((0, 1))
    lax.fori_loop(PAGES, 2 * PAGES, take_page, 0)
    stage_b((2, 3))
    for load in loads:
        load.wait()
    gathered(0)
    project(0)
    stage_c((2, 3))
    stage_a((4,))
    gathered(1)
    project(1)
    stage_d((2, 3))
    stage_b((4,))
    gathered(2)
    project(2)
    stage_c((4,))
    stage_a((5,))
    gathered(3)
    project(3)
    stage_d((4,))
    stage_b((5,))
    some_heads(attend, 0, 0, 2)
    stage_c((5,))
    gathered(4)
    project(4)
    stage_d((5,))
    some_heads(attend, 0, 2, HEADS_HERE)
    give(0).start()
    some_heads(attend_early, 1, 0, HEADS_HERE)
    gathered(5)
    lay_out(5)
    last_columns(0)
    last_columns(2)
    attend_late(1, 0)
    last_columns(1)
    attend_late(1, 1)
    last_columns(3)
    attend_late(1, 2)
    attend_late(1, 3)
    give(1).start()
    for pair in range(CHUNKS // 2):
        all_left(pair)
    give(0).wait()
    give(1).wait()


def body(prefix_store, page_owner, prefix_len, turn_rows, turn_len, w_query, w_key, w_value):
    smem = pl.BlockSpec(memory_space=pltpu.SMEM)
    hbm = pl.BlockSpec(memory_space=pl.ANY)
    return pl.pallas_call(
        kernel,
        out_shape=jax.ShapeDtypeStruct((CONVS, TURN, COLS), BF),
        in_specs=[smem, smem, smem, hbm, hbm, hbm, hbm, hbm],
        out_specs=hbm,
        scratch_shapes=[
            pltpu.VMEM((GROUPS, SLICE, PAGE), BF),
            pltpu.VMEM((CONVS, TURN, COLS), BF),
            pltpu.VMEM((HEADS_HERE, TURN, 128), F32),
            pltpu.VMEM((HEADS_HERE, TURN, 128), F32),
            pltpu.VMEM((HEADS_HERE, TURN, HS), F32),
            pltpu.VMEM((CHUNKS, TP, SLICE, 128), BF),
            pltpu.VMEM((GROUPS, 2, SLICE, PAGE), BF),
            pltpu.VMEM((GROUPS, 2, SLICE, PAGE), BF),
            pltpu.VMEM((WIDTH, 3 * COLS), BF),
            pltpu.VMEM((2 * PAGE, WIDTH), BF),
            pltpu.VMEM((CONVS, TURN, 3 * COLS), BF),
            pltpu.VMEM((CONVS, PREFIX, 2 * COLS), BF),
            pltpu.SemaphoreType.DMA((TURN_CHUNKS + 1,)),
            pltpu.SemaphoreType.DMA((CONVS,)),
            pltpu.SemaphoreType.DMA((3,)),
            pltpu.SemaphoreType.DMA((GROUPS,)),
            pltpu.SemaphoreType.DMA((GROUPS,)),
            pltpu.SemaphoreType.DMA((CHUNKS,)),
            pltpu.SemaphoreType.DMA((CHUNKS, TP, 2)),
        ],
        compiler_params=pltpu.CompilerParams(
            collective_id=0, has_side_effects=True, vmem_limit_bytes=63 * 2**20
        ),
        cost_estimate=pl.CostEstimate(
            flops=27_000_000_000, bytes_accessed=26_000_000, transcendentals=1_600_000
        ),
        name="resume_attention",
    )(
        page_owner.T,
        prefix_len,
        turn_len,
        jnp.swapaxes(prefix_store, 1, 2),
        jnp.swapaxes(turn_rows, 1, 2),
        w_query,
        w_key,
        w_value,
    )


def solution(mesh):
    in_specs = (
        P("group", None, "tp"),
        P(),
        P("group"),
        P("group", None, "tp"),
        P("group"),
        P(None, "tp"),
        P(None, "tp"),
        P(None, "tp"),
    )
    out_specs = P("group", None, "tp")
    return jax.shard_map(body, mesh=mesh, in_specs=in_specs, out_specs=out_specs, check_vma=False)
```

```python
import functools

import jax
import jax.numpy as jnp
from jax import lax
from jax.experimental import pallas as pl
from jax.experimental.pallas import tpu as pltpu
from jax.sharding import PartitionSpec as P

MESH = pl.DeviceIdType.MESH

SIDE = 4
TP = SIDE * SIDE
GROUPS = 8
HS = 128
HEADS_HERE = 4
COLS = HEADS_HERE * HS
WIDTH = 7168
SLICE = WIDTH // TP
PAGE = 128
PAGES = 4
CONVS = 2
TURN = 256
PREFIX = 512
PART = SLICE // 2
SENT = 15
TURN_CHUNKS = CONVS * TURN // PAGE
CHUNKS = TURN_CHUNKS + CONVS * PAGES
WIDE = 256
FIRST_HEAD = 48.0
ALL_HEADS = 112.0
BF = jnp.bfloat16
F32 = jnp.float32


def kernel(
    owner_ref,
    prefix_len_ref,
    turn_len_ref,
    store_hbm,
    turn_hbm,
    wq_ref,
    wk_ref,
    wv_ref,
    out_hbm,
    store_ref,
    out_ref,
    part_top,
    part_sum,
    part_context,
    held,
    pages_out,
    pages_in,
    weight,
    whole,
    from_turn,
    from_prefix,
    own_sem,
    out_sem,
    weight_sem,
    page_send,
    page_recv,
    send_sem,
    recv_sem,
):
    group = lax.axis_index("group")
    tp = lax.axis_index("tp")
    y, z = tp // SIDE, tp % SIDE

    neighbour = [
        [((y + 1) % SIDE) * SIDE + z, ((y + SIDE - 1) % SIDE) * SIDE + z],
        [y * SIDE + (z + 1) % SIDE, y * SIDE + (z + SIDE - 1) % SIDE],
    ]

    fetch_turn = [
        pltpu.make_async_copy(
            turn_hbm.at[chunk // 2, :, pl.ds((chunk % 2) * PAGE, PAGE)],
            held.at[chunk, 0],
            own_sem.at[chunk],
        )
        for chunk in range(TURN_CHUNKS)
    ]
    fetch_store = pltpu.make_async_copy(store_hbm, store_ref, own_sem.at[TURN_CHUNKS])
    for fetch in fetch_turn:
        fetch.start()
    fetch_store.start()

    barrier = pltpu.get_barrier_semaphore()
    for axis in range(2):
        for way in range(2):
            pl.semaphore_signal(
                barrier, inc=1, device_id=(group, neighbour[axis][way]), device_id_type=MESH
            )
    for off in range(1, GROUPS):
        pl.semaphore_signal(
            barrier, inc=1, device_id=((group + off) % GROUPS, tp), device_id_type=MESH
        )

    loads = [
        pltpu.make_async_copy(source, weight.at[:, pl.ds(i * COLS, COLS)], weight_sem.at[i])
        for i, source in enumerate((wq_ref, wk_ref, wv_ref))
    ]
    for fetch in fetch_turn:
        fetch.wait()
    pl.semaphore_wait(barrier, 4 + GROUPS - 1)

    def copy(chunk, source, target, axis, way, half, stage):
        part = pl.ds(0, SLICE) if half is None else pl.ds(half * PART, PART)
        return pltpu.make_async_remote_copy(
            src_ref=held.at[chunk, source, part],
            dst_ref=held.at[chunk, target, part],
            send_sem=send_sem.at[chunk],
            recv_sem=recv_sem.at[chunk, stage],
            device_id=(group, neighbour[axis][way]),
            device_id_type=MESH,
        )

    def chunks_of(pair):
        return [(2 * pair, 0), (2 * pair + 1, 1)]

    def near_first(pair):
        return [
            copy(chunk, 0, (3 - 2 * way) * SIDE, axis, way, None, 0)
            for chunk, axis in chunks_of(pair)
            for way in range(2)
        ]

    def far_first(pair):
        return [
            copy(chunk, (3 - 2 * way) * SIDE, 2 * SIDE, axis, way, way, 1)
            for chunk, axis in chunks_of(pair)
            for way in range(2)
        ]

    def near_second(pair, which):
        return [
            copy(chunk, i * SIDE, i * SIDE + 3 - 2 * way, 1 - axis, way, None, (2, 3, 4, 3)[i])
            for i in which
            for chunk, axis in chunks_of(pair)
            for way in range(2)
        ]

    def far_second(pair, which):
        return [
            copy(chunk, i * SIDE + 3 - 2 * way, i * SIDE + 2, 1 - axis, way, way, 5)
            for i in which
            for chunk, axis in chunks_of(pair)
            for way in range(2)
        ]

    def start(copies):
        for one in copies:
            one.start()

    def arrived(pair, stage, count):
        for chunk, axis in chunks_of(pair):
            blocks = held.at[chunk, pl.ds(0, count)]
            pltpu.make_async_remote_copy(
                src_ref=blocks,
                dst_ref=blocks,
                send_sem=send_sem.at[chunk],
                recv_sem=recv_sem.at[chunk, stage],
                device_id=(group, neighbour[axis][0]),
                device_id_type=MESH,
            ).wait_recv()

    def stage_a(pairs):
        for pair in pairs:
            start(near_first(pair))
        for pair in pairs:
            start(near_second(pair, (0,)))

    def stage_b(pairs):
        for pair in pairs:
            arrived(pair, 0, 2)
            start(far_first(pair))
            start(near_second(pair, (1, 3)))

    def stage_c(pairs):
        for pair in pairs:
            arrived(pair, 1, 1)
            start(near_second(pair, (2,)))
            arrived(pair, 2, 2)
            start(far_second(pair, (0,)))

    def stage_d(pairs):
        for pair in pairs:
            arrived(pair, 3, 4)
            start(far_second(pair, (1, 3)))
        for pair in pairs:
            arrived(pair, 4, 2)
            start(far_second(pair, (2,)))

    def gathered(pair):
        arrived(pair, 5, 4)

    def all_left(pair):
        for chunk, axis in chunks_of(pair):
            blocks = held.at[chunk, pl.ds(0, SENT)]
            pltpu.make_async_remote_copy(
                src_ref=blocks,
                dst_ref=blocks,
                send_sem=send_sem.at[chunk],
                recv_sem=recv_sem.at[chunk, 0],
                device_id=(group, neighbour[axis][0]),
                device_id_type=MESH,
            ).wait_send()

    def owner(page):
        return owner_ref[page % PAGES, page // PAGES]

    def stage_pages(to, carry):
        found = jnp.int32(0)
        first = jnp.int32(0)
        second = jnp.int32(0)
        for j in range(CONVS * PAGES):
            slot = owner(to * (CONVS * PAGES) + j)
            mine = slot // GROUPS == group
            first = jnp.where(mine & (found == 0), slot % GROUPS, first)
            second = jnp.where(mine & (found == 1), slot % GROUPS, second)
            found = found + mine.astype(jnp.int32)
        pages_out[to, 0] = store_ref[first]
        pages_out[to, 1] = store_ref[second]
        return carry

    def exchange(off, at):
        return pltpu.make_async_remote_copy(
            src_ref=pages_out.at[(group + off) % GROUPS],
            dst_ref=pages_in.at[at],
            send_sem=page_send.at[off],
            recv_sem=page_recv.at[off],
            device_id=((group + off) % GROUPS, tp),
            device_id_type=MESH,
        )

    def take_page(i, carry):
        source = owner(group * (CONVS * PAGES) + i) // GROUPS
        earlier = jnp.int32(0)
        for j in range(CONVS * PAGES):
            same = owner(group * (CONVS * PAGES) + j) // GROUPS == source
            earlier = earlier + (same & (j < i)).astype(jnp.int32)
        held[TURN_CHUNKS + i, 0] = pages_in[source, jnp.minimum(earlier, 1)]
        return carry

    def lay_out(pair):
        def two(v, carry):
            def slot_of(device, axis):
                on_y = (device // SIDE - y + SIDE) % SIDE
                on_z = (device % SIDE - z + SIDE) % SIDE
                return on_y * SIDE + on_z if axis == 0 else on_z * SIDE + on_y

            at = pl.ds(pl.multiple_of(v * (2 * SLICE), 128), 2 * SLICE)
            for chunk, axis in chunks_of(pair):
                blocks = [held[chunk, slot_of(2 * v + k, axis)] for k in range(2)]
                whole[pl.ds(axis * PAGE, PAGE), at] = jnp.concatenate(blocks, axis=0).T
            return carry

        lax.fori_loop(0, TP // 2, two, 0)

    def project(pair):
        lay_out(pair)

        def turn_columns(n, carry):
            at = pl.ds(pl.multiple_of(n * WIDE, WIDE), WIDE)
            term = jnp.dot(whole[...], weight[:, at], preferred_element_type=F32)
            from_turn[pair, :, at] = term.astype(BF)
            return carry

        def prefix_columns(n, carry):
            at = pl.ds(pl.multiple_of(n * WIDE, WIDE), WIDE)
            of = pl.ds(pl.multiple_of(COLS + n * WIDE, WIDE), WIDE)
            term = jnp.dot(whole[...], weight[:, of], preferred_element_type=F32)
            conv, half = (pair - CONVS) // 2, (pair - CONVS) % 2
            from_prefix[conv, pl.ds(half * WIDE, WIDE), at] = term.astype(BF)
            return carry

        if pair < CONVS:
            lax.fori_loop(0, 3 * COLS // WIDE, turn_columns, 0)
        else:
            lax.fori_loop(0, 2 * COLS // WIDE, prefix_columns, 0)

    def last_columns(n):
        of = pl.ds(COLS + n * WIDE, WIDE)
        term = jnp.dot(whole[...], weight[:, of], preferred_element_type=F32)
        from_prefix[CONVS - 1, pl.ds(WIDE, WIDE), pl.ds(n * WIDE, WIDE)] = term.astype(BF)

    def slope_of(head):
        number = jnp.asarray(tp * HEADS_HERE + head, F32)
        power = jnp.full((1, 128), 1.0, F32) * (-8.0 * (FIRST_HEAD + 1.0 + number) / ALL_HEADS)
        return jnp.exp2(power)[:, :1]

    def columns(which, head):
        if isinstance(head, int):
            return pl.ds(which * COLS + head * HS, HS)
        return pl.ds(pl.multiple_of(which * COLS + head * HS, HS), HS)

    def dots(left_side, right_side):
        return lax.dot_general(
            left_side, right_side, (((1,), (1,)), ((), ())), preferred_element_type=F32
        ) * (HS**-0.5)

    def prefix_scores(conv, head, lo, count):
        scores = dots(
            from_turn[conv, :, columns(0, head)], from_prefix[conv, pl.ds(lo, count), columns(0, head)]
        )
        i = lax.broadcasted_iota(jnp.int32, (TURN, count), 0)
        j = lax.broadcasted_iota(jnp.int32, (TURN, count), 1) + lo
        away = (prefix_len_ref[conv] + i - j).astype(F32)
        return jnp.where(j < prefix_len_ref[conv], scores - slope_of(head) * away, -jnp.inf)

    def turn_scores(conv, head):
        scores = dots(from_turn[conv, :, columns(0, head)], from_turn[conv, :, columns(1, head)])
        i = lax.broadcasted_iota(jnp.int32, (TURN, TURN), 0)
        j = lax.broadcasted_iota(jnp.int32, (TURN, TURN), 1)
        away = (i - j).astype(F32)
        live = j < jnp.minimum(i + 1, turn_len_ref[conv])
        return jnp.where(live, scores - slope_of(head) * away, -jnp.inf)

    def highest(scores):
        return jnp.max(scores, axis=1, keepdims=True)

    def summed(scores):
        return jnp.sum(scores, axis=1, keepdims=True)

    def prefix_values(conv, head, lo, count, weights):
        return jnp.dot(
            weights.astype(BF),
            from_prefix[conv, pl.ds(lo, count), columns(1, head)],
            preferred_element_type=F32,
        )

    def turn_values(conv, head, weights):
        return jnp.dot(
            weights.astype(BF), from_turn[conv, :, columns(2, head)], preferred_element_type=F32
        )

    def attend(conv, head):
        on_prefix, on_turn = prefix_scores(conv, head, 0, PREFIX), turn_scores(conv, head)
        top = jnp.maximum(highest(on_prefix), highest(on_turn))
        on_prefix, on_turn = jnp.exp(on_prefix - top), jnp.exp(on_turn - top)
        share = 1.0 / (summed(on_prefix) + summed(on_turn))
        context = prefix_values(conv, head, 0, PREFIX, on_prefix * share)
        context = context + turn_values(conv, head, on_turn * share)
        out_ref[conv, :, columns(0, head)] = context.astype(BF)

    def attend_early(conv, head):
        on_prefix, on_turn = prefix_scores(conv, head, 0, PREFIX // 2), turn_scores(conv, head)
        top = jnp.maximum(highest(on_prefix), highest(on_turn))
        on_prefix, on_turn = jnp.exp(on_prefix - top), jnp.exp(on_turn - top)
        part_top[head] = jnp.broadcast_to(top, (TURN, 128))
        part_sum[head] = jnp.broadcast_to(summed(on_prefix) + summed(on_turn), (TURN, 128))
        part_context[head] = prefix_values(conv, head, 0, PREFIX // 2, on_prefix) + turn_values(
            conv, head, on_turn
        )

    def attend_late(conv, head):
        on_prefix = prefix_scores(conv, head, PREFIX // 2, PREFIX // 2)
        early_top = part_top[head, :, :1]
        top = jnp.maximum(early_top, highest(on_prefix))
        on_prefix = jnp.exp(on_prefix - top)
        kept = jnp.exp(early_top - top)
        total = part_sum[head, :, :1] * kept + summed(on_prefix)
        context = part_context[head] * kept + prefix_values(
            conv, head, PREFIX // 2, PREFIX // 2, on_prefix
        )
        out_ref[conv, :, columns(0, head)] = (context * (1.0 / total)).astype(BF)

    def some_heads(attention, conv, lo, hi):
        def one(head, carry):
            attention(conv, head)
            return carry

        lax.fori_loop(lo, hi, one, 0)

    def give(conv):
        return pltpu.make_async_copy(out_ref.at[conv], out_hbm.at[conv], out_sem.at[conv])

    stage_a((0, 1))
    fetch_store.wait()
    lax.fori_loop(0, GROUPS, stage_pages, 0)
    for off in range(1, GROUPS):
        exchange(off, group).start()
    for load in loads:
        load.start()
    pages_in[group] = pages_out[group]
    stage_b((0, 1))
    stage_c((0, 1))
    for off in range(1, GROUPS):
        exchange(off, (group - off + GROUPS) % GROUPS).wait()
    lax.fori_loop(0, PAGES, take_page, 0)
    stage_a((2, 3))
    stage_d((0, 1))
    lax.fori_loop(PAGES, 2 * PAGES, take_page, 0)
    stage_b((2, 3))
    for load in loads:
        load.wait()
    gathered(0)
    project(0)
    stage_c((2, 3))
    stage_a((4,))
    gathered(1)
    project(1)
    stage_d((2, 3))
    stage_b((4,))
    gathered(2)
    project(2)
    stage_c((4,))
    stage_a((5,))
    gathered(3)
    project(3)
    stage_d((4,))
    stage_b((5,))
    some_heads(attend, 0, 0, 2)
    stage_c((5,))
    gathered(4)
    project(4)
    stage_d((5,))
    some_heads(attend, 0, 2, HEADS_HERE)
    give(0).start()
    some_heads(attend_early, 1, 0, HEADS_HERE)
    gathered(5)
    lay_out(5)
    last_columns(0)
    last_columns(2)
    attend_late(1, 0)
    last_columns(1)
    attend_late(1, 1)
    last_columns(3)
    attend_late(1, 2)
    attend_late(1, 3)
    give(1).start()
    for pair in range(CHUNKS // 2):
        all_left(pair)
    give(0).wait()
    give(1).wait()


def body(prefix_store, page_owner, prefix_len, turn_rows, turn_len, w_query, w_key, w_value):
    smem = pl.BlockSpec(memory_space=pltpu.SMEM)
    hbm = pl.BlockSpec(memory_space=pl.ANY)
    return pl.pallas_call(
        kernel,
        out_shape=jax.ShapeDtypeStruct((CONVS, TURN, COLS), BF),
        in_specs=[smem, smem, smem, hbm, hbm, hbm, hbm, hbm],
        out_specs=hbm,
        scratch_shapes=[
            pltpu.VMEM((GROUPS, SLICE, PAGE), BF),
            pltpu.VMEM((CONVS, TURN, COLS), BF),
            pltpu.VMEM((HEADS_HERE, TURN, 128), F32),
            pltpu.VMEM((HEADS_HERE, TURN, 128), F32),
            pltpu.VMEM((HEADS_HERE, TURN, HS), F32),
            pltpu.VMEM((CHUNKS, TP, SLICE, 128), BF),
            pltpu.VMEM((GROUPS, 2, SLICE, PAGE), BF),
            pltpu.VMEM((GROUPS, 2, SLICE, PAGE), BF),
            pltpu.VMEM((WIDTH, 3 * COLS), BF),
            pltpu.VMEM((2 * PAGE, WIDTH), BF),
            pltpu.VMEM((CONVS, TURN, 3 * COLS), BF),
            pltpu.VMEM((CONVS, PREFIX, 2 * COLS), BF),
            pltpu.SemaphoreType.DMA((TURN_CHUNKS + 1,)),
            pltpu.SemaphoreType.DMA((CONVS,)),
            pltpu.SemaphoreType.DMA((3,)),
            pltpu.SemaphoreType.DMA((GROUPS,)),
            pltpu.SemaphoreType.DMA((GROUPS,)),
            pltpu.SemaphoreType.DMA((CHUNKS,)),
            pltpu.SemaphoreType.DMA((CHUNKS, 6)),
        ],
        compiler_params=pltpu.CompilerParams(
            collective_id=0, has_side_effects=True, vmem_limit_bytes=63 * 2**20
        ),
        cost_estimate=pl.CostEstimate(
            flops=27_000_000_000, bytes_accessed=26_000_000, transcendentals=1_600_000
        ),
        name="resume_attention",
    )(
        page_owner.T,
        prefix_len,
        turn_len,
        jnp.swapaxes(prefix_store, 1, 2),
        jnp.swapaxes(turn_rows, 1, 2),
        w_query,
        w_key,
        w_value,
    )


def solution(mesh):
    in_specs = (
        P("group", None, "tp"),
        P(),
        P("group"),
        P("group", None, "tp"),
        P("group"),
        P(None, "tp"),
        P(None, "tp"),
        P(None, "tp"),
    )
    out_specs = P("group", None, "tp")
    return jax.shard_map(body, mesh=mesh, in_specs=in_specs, out_specs=out_specs, check_vma=False)
```

```python
import functools

import jax
import jax.numpy as jnp
from jax import lax
from jax.experimental import pallas as pl
from jax.experimental.pallas import tpu as pltpu
from jax.sharding import PartitionSpec as P

MESH = pl.DeviceIdType.MESH

SIDE = 4
TP = SIDE * SIDE
GROUPS = 8
HS = 128
HEADS_HERE = 4
COLS = HEADS_HERE * HS
WIDTH = 7168
SLICE = WIDTH // TP
PAGE = 128
PAGES = 4
CONVS = 2
TURN = 256
PREFIX = 512
PART = SLICE // 2
SENT = 15
TURN_CHUNKS = CONVS * TURN // PAGE
CHUNKS = TURN_CHUNKS + CONVS * PAGES
WIDE = 256
FIRST_HEAD = 48.0
ALL_HEADS = 112.0
BF = jnp.bfloat16
F32 = jnp.float32


def kernel(
    owner_ref,
    prefix_len_ref,
    turn_len_ref,
    store_hbm,
    turn_hbm,
    wq_ref,
    wk_ref,
    wv_ref,
    out_hbm,
    store_ref,
    out_ref,
    part_top,
    part_sum,
    part_context,
    held,
    pages_out,
    pages_in,
    weight,
    whole,
    from_turn,
    from_prefix,
    own_sem,
    out_sem,
    weight_sem,
    page_send,
    page_recv,
    send_sem,
    recv_sem,
):
    group = lax.axis_index("group")
    tp = lax.axis_index("tp")
    y, z = tp // SIDE, tp % SIDE

    neighbour = [
        [((y + 1) % SIDE) * SIDE + z, ((y + SIDE - 1) % SIDE) * SIDE + z],
        [y * SIDE + (z + 1) % SIDE, y * SIDE + (z + SIDE - 1) % SIDE],
    ]

    fetch_turn = [
        pltpu.make_async_copy(
            turn_hbm.at[chunk // 2, :, pl.ds((chunk % 2) * PAGE, PAGE)],
            held.at[chunk, 0],
            own_sem.at[chunk],
        )
        for chunk in range(TURN_CHUNKS)
    ]
    fetch_store = pltpu.make_async_copy(store_hbm, store_ref, own_sem.at[TURN_CHUNKS])
    for fetch in fetch_turn:
        fetch.start()
    fetch_store.start()

    barrier = pltpu.get_barrier_semaphore()
    for axis in range(2):
        for way in range(2):
            pl.semaphore_signal(
                barrier, inc=1, device_id=(group, neighbour[axis][way]), device_id_type=MESH
            )
    for off in range(1, GROUPS):
        pl.semaphore_signal(
            barrier, inc=1, device_id=((group + off) % GROUPS, tp), device_id_type=MESH
        )

    loads = [
        pltpu.make_async_copy(source, weight.at[:, pl.ds(i * COLS, COLS)], weight_sem.at[i])
        for i, source in enumerate((wq_ref, wk_ref, wv_ref))
    ]
    for fetch in fetch_turn:
        fetch.wait()
    pl.semaphore_wait(barrier, 4 + GROUPS - 1)

    def copy(chunk, source, target, axis, way, half, stage):
        part = pl.ds(0, SLICE) if half is None else pl.ds(half * PART, PART)
        return pltpu.make_async_remote_copy(
            src_ref=held.at[chunk, source, part],
            dst_ref=held.at[chunk, target, part],
            send_sem=send_sem.at[chunk],
            recv_sem=recv_sem.at[chunk, stage],
            device_id=(group, neighbour[axis][way]),
            device_id_type=MESH,
        )

    def chunks_of(pair):
        return [(2 * pair, 0), (2 * pair + 1, 1)]

    def near_first(pair):
        return [
            copy(chunk, 0, (3 - 2 * way) * SIDE, axis, way, None, 0)
            for chunk, axis in chunks_of(pair)
            for way in range(2)
        ]

    def far_first(pair):
        return [
            copy(chunk, (3 - 2 * way) * SIDE, 2 * SIDE, axis, way, way, 1)
            for chunk, axis in chunks_of(pair)
            for way in range(2)
        ]

    def near_second(pair, which):
        return [
            copy(chunk, i * SIDE, i * SIDE + 3 - 2 * way, 1 - axis, way, None, (2, 3, 4, 3)[i])
            for i in which
            for chunk, axis in chunks_of(pair)
            for way in range(2)
        ]

    def far_second(pair, which):
        return [
            copy(chunk, i * SIDE + 3 - 2 * way, i * SIDE + 2, 1 - axis, way, way, 5)
            for i in which
            for chunk, axis in chunks_of(pair)
            for way in range(2)
        ]

    def start(copies):
        for one in copies:
            one.start()

    def arrived(pair, stage, count):
        for chunk, axis in chunks_of(pair):
            blocks = held.at[chunk, pl.ds(0, count)]
            pltpu.make_async_remote_copy(
                src_ref=blocks,
                dst_ref=blocks,
                send_sem=send_sem.at[chunk],
                recv_sem=recv_sem.at[chunk, stage],
                device_id=(group, neighbour[axis][0]),
                device_id_type=MESH,
            ).wait_recv()

    def stage_a(pairs):
        for pair in pairs:
            start(near_first(pair))
        for pair in pairs:
            start(near_second(pair, (0,)))

    def stage_b(pairs):
        for pair in pairs:
            arrived(pair, 0, 2)
            start(far_first(pair))
            start(near_second(pair, (1, 3)))

    def stage_c(pairs):
        for pair in pairs:
            arrived(pair, 1, 1)
            start(near_second(pair, (2,)))
            arrived(pair, 2, 2)
            start(far_second(pair, (0,)))

    def stage_d(pairs):
        for pair in pairs:
            arrived(pair, 3, 4)
            start(far_second(pair, (1, 3)))
        for pair in pairs:
            arrived(pair, 4, 2)
            start(far_second(pair, (2,)))

    def gathered(pair):
        arrived(pair, 5, 4)

    def all_left(pair):
        for chunk, axis in chunks_of(pair):
            blocks = held.at[chunk, pl.ds(0, SENT)]
            pltpu.make_async_remote_copy(
                src_ref=blocks,
                dst_ref=blocks,
                send_sem=send_sem.at[chunk],
                recv_sem=recv_sem.at[chunk, 0],
                device_id=(group, neighbour[axis][0]),
                device_id_type=MESH,
            ).wait_send()

    def owner(page):
        return owner_ref[page % PAGES, page // PAGES]

    def stage_pages(to, carry):
        found = jnp.int32(0)
        first = jnp.int32(0)
        second = jnp.int32(0)
        for j in range(CONVS * PAGES):
            slot = owner(to * (CONVS * PAGES) + j)
            mine = slot // GROUPS == group
            first = jnp.where(mine & (found == 0), slot % GROUPS, first)
            second = jnp.where(mine & (found == 1), slot % GROUPS, second)
            found = found + mine.astype(jnp.int32)
        pages_out[to, 0] = store_ref[first]
        pages_out[to, 1] = store_ref[second]
        return carry

    def exchange(off, at):
        return pltpu.make_async_remote_copy(
            src_ref=pages_out.at[(group + off) % GROUPS],
            dst_ref=pages_in.at[at],
            send_sem=page_send.at[off],
            recv_sem=page_recv.at[off],
            device_id=((group + off) % GROUPS, tp),
            device_id_type=MESH,
        )

    def take_page(i, carry):
        source = owner(group * (CONVS * PAGES) + i) // GROUPS
        earlier = jnp.int32(0)
        for j in range(CONVS * PAGES):
            same = owner(group * (CONVS * PAGES) + j) // GROUPS == source
            earlier = earlier + (same & (j < i)).astype(jnp.int32)
        held[TURN_CHUNKS + i, 0] = pages_in[source, jnp.minimum(earlier, 1)]
        return carry

    def lay_two(chunk, axis, v):
        def slot_of(device):
            on_y = (device // SIDE - y + SIDE) % SIDE
            on_z = (device % SIDE - z + SIDE) % SIDE
            return on_y * SIDE + on_z if axis == 0 else on_z * SIDE + on_y

        at = pl.ds(pl.multiple_of(v * (2 * SLICE), 128), 2 * SLICE)
        blocks = [held[chunk, slot_of(2 * v + k)] for k in range(2)]
        whole[pl.ds(axis * PAGE, PAGE), at] = jnp.concatenate(blocks, axis=0).T

    def lay_early(pair):
        for chunk, axis in chunks_of(pair):
            for n in range(4 if axis == 0 else 6):
                if axis == 0:
                    lay_two(chunk, axis, 2 * n + 1 - (z + 2) % SIDE // 2)
                else:
                    lay_two(chunk, axis, 2 * ((y + 3 + n // 2) % SIDE) + n % 2)

    def lay_late(pair):
        for chunk, axis in chunks_of(pair):
            for n in range(4 if axis == 0 else 2):
                if axis == 0:
                    lay_two(chunk, axis, 2 * n + (z + 2) % SIDE // 2)
                else:
                    lay_two(chunk, axis, 2 * ((y + 2) % SIDE) + n)

    def lay_out(pair):
        def two(v, carry):
            for chunk, axis in chunks_of(pair):
                lay_two(chunk, axis, v)
            return carry

        lax.fori_loop(0, TP // 2, two, 0)

    def project(pair):
        lay_out(pair)

        def turn_columns(n, carry):
            at = pl.ds(pl.multiple_of(n * WIDE, WIDE), WIDE)
            term = jnp.dot(whole[...], weight[:, at], preferred_element_type=F32)
            from_turn[pair, :, at] = term.astype(BF)
            return carry

        def prefix_columns(n, carry):
            at = pl.ds(pl.multiple_of(n * WIDE, WIDE), WIDE)
            of = pl.ds(pl.multiple_of(COLS + n * WIDE, WIDE), WIDE)
            term = jnp.dot(whole[...], weight[:, of], preferred_element_type=F32)
            conv, half = (pair - CONVS) // 2, (pair - CONVS) % 2
            from_prefix[conv, pl.ds(half * WIDE, WIDE), at] = term.astype(BF)
            return carry

        if pair < CONVS:
            lax.fori_loop(0, 3 * COLS // WIDE, turn_columns, 0)
        else:
            lax.fori_loop(0, 2 * COLS // WIDE, prefix_columns, 0)

    def last_columns(n):
        of = pl.ds(COLS + n * WIDE, WIDE)
        term = jnp.dot(whole[...], weight[:, of], preferred_element_type=F32)
        from_prefix[CONVS - 1, pl.ds(WIDE, WIDE), pl.ds(n * WIDE, WIDE)] = term.astype(BF)

    def slope_of(head):
        number = jnp.asarray(tp * HEADS_HERE + head, F32)
        power = jnp.full((1, 128), 1.0, F32) * (-8.0 * (FIRST_HEAD + 1.0 + number) / ALL_HEADS)
        return jnp.exp2(power)[:, :1]

    def columns(which, head):
        if isinstance(head, int):
            return pl.ds(which * COLS + head * HS, HS)
        return pl.ds(pl.multiple_of(which * COLS + head * HS, HS), HS)

    def dots(left_side, right_side):
        return lax.dot_general(
            left_side, right_side, (((1,), (1,)), ((), ())), preferred_element_type=F32
        ) * (HS**-0.5)

    def prefix_scores(conv, head, lo, count):
        scores = dots(
            from_turn[conv, :, columns(0, head)], from_prefix[conv, pl.ds(lo, count), columns(0, head)]
        )
        i = lax.broadcasted_iota(jnp.int32, (TURN, count), 0)
        j = lax.broadcasted_iota(jnp.int32, (TURN, count), 1) + lo
        away = (prefix_len_ref[conv] + i - j).astype(F32)
        return jnp.where(j < prefix_len_ref[conv], scores - slope_of(head) * away, -jnp.inf)

    def turn_scores(conv, head):
        scores = dots(from_turn[conv, :, columns(0, head)], from_turn[conv, :, columns(1, head)])
        i = lax.broadcasted_iota(jnp.int32, (TURN, TURN), 0)
        j = lax.broadcasted_iota(jnp.int32, (TURN, TURN), 1)
        away = (i - j).astype(F32)
        live = j < jnp.minimum(i + 1, turn_len_ref[conv])
        return jnp.where(live, scores - slope_of(head) * away, -jnp.inf)

    def highest(scores):
        return jnp.max(scores, axis=1, keepdims=True)

    def summed(scores):
        return jnp.sum(scores, axis=1, keepdims=True)

    def prefix_values(conv, head, lo, count, weights):
        return jnp.dot(
            weights.astype(BF),
            from_prefix[conv, pl.ds(lo, count), columns(1, head)],
            preferred_element_type=F32,
        )

    def turn_values(conv, head, weights):
        return jnp.dot(
            weights.astype(BF), from_turn[conv, :, columns(2, head)], preferred_element_type=F32
        )

    def attend(conv, head):
        on_prefix, on_turn = prefix_scores(conv, head, 0, PREFIX), turn_scores(conv, head)
        top = jnp.maximum(highest(on_prefix), highest(on_turn))
        on_prefix, on_turn = jnp.exp(on_prefix - top), jnp.exp(on_turn - top)
        share = 1.0 / (summed(on_prefix) + summed(on_turn))
        context = prefix_values(conv, head, 0, PREFIX, on_prefix * share)
        context = context + turn_values(conv, head, on_turn * share)
        out_ref[conv, :, columns(0, head)] = context.astype(BF)

    def attend_early(conv, head):
        on_prefix, on_turn = prefix_scores(conv, head, 0, PREFIX // 2), turn_scores(conv, head)
        top = jnp.maximum(highest(on_prefix), highest(on_turn))
        on_prefix, on_turn = jnp.exp(on_prefix - top), jnp.exp(on_turn - top)
        part_top[head] = jnp.broadcast_to(top, (TURN, 128))
        part_sum[head] = jnp.broadcast_to(summed(on_prefix) + summed(on_turn), (TURN, 128))
        part_context[head] = prefix_values(conv, head, 0, PREFIX // 2, on_prefix) + turn_values(
            conv, head, on_turn
        )

    def attend_late(conv, head):
        on_prefix = prefix_scores(conv, head, PREFIX // 2, PREFIX // 2)
        early_top = part_top[head, :, :1]
        top = jnp.maximum(early_top, highest(on_prefix))
        on_prefix = jnp.exp(on_prefix - top)
        kept = jnp.exp(early_top - top)
        total = part_sum[head, :, :1] * kept + summed(on_prefix)
        context = part_context[head] * kept + prefix_values(
            conv, head, PREFIX // 2, PREFIX // 2, on_prefix
        )
        out_ref[conv, :, columns(0, head)] = (context * (1.0 / total)).astype(BF)

    def some_heads(attention, conv, lo, hi):
        def one(head, carry):
            attention(conv, head)
            return carry

        lax.fori_loop(lo, hi, one, 0)

    def give(conv):
        return pltpu.make_async_copy(out_ref.at[conv], out_hbm.at[conv], out_sem.at[conv])

    stage_a((0, 1))
    fetch_store.wait()
    lax.fori_loop(0, GROUPS, stage_pages, 0)
    for off in range(1, GROUPS):
        exchange(off, group).start()
    for load in loads:
        load.start()
    pages_in[group] = pages_out[group]
    stage_b((0, 1))
    stage_c((0, 1))
    for off in range(1, GROUPS):
        exchange(off, (group - off + GROUPS) % GROUPS).wait()
    lax.fori_loop(0, PAGES, take_page, 0)
    stage_a((2, 3))
    stage_d((0, 1))
    lax.fori_loop(PAGES, 2 * PAGES, take_page, 0)
    stage_b((2, 3))
    for load in loads:
        load.wait()
    gathered(0)
    project(0)
    stage_c((2, 3))
    stage_a((4,))
    gathered(1)
    project(1)
    stage_d((2, 3))
    stage_b((4,))
    gathered(2)
    project(2)
    stage_c((4,))
    stage_a((5,))
    gathered(3)
    project(3)
    stage_d((4,))
    stage_b((5,))
    some_heads(attend, 0, 0, 2)
    stage_c((5,))
    gathered(4)
    project(4)
    stage_d((5,))
    some_heads(attend, 0, 2, HEADS_HERE)
    give(0).start()
    some_heads(attend_early, 1, 0, HEADS_HERE)
    lay_early(5)
    gathered(5)
    lay_late(5)
    last_columns(0)
    last_columns(2)
    attend_late(1, 0)
    last_columns(1)
    attend_late(1, 1)
    last_columns(3)
    attend_late(1, 2)
    attend_late(1, 3)
    give(1).start()
    for pair in range(CHUNKS // 2):
        all_left(pair)
    give(0).wait()
    give(1).wait()


def body(prefix_store, page_owner, prefix_len, turn_rows, turn_len, w_query, w_key, w_value):
    smem = pl.BlockSpec(memory_space=pltpu.SMEM)
    hbm = pl.BlockSpec(memory_space=pl.ANY)
    return pl.pallas_call(
        kernel,
        out_shape=jax.ShapeDtypeStruct((CONVS, TURN, COLS), BF),
        in_specs=[smem, smem, smem, hbm, hbm, hbm, hbm, hbm],
        out_specs=hbm,
        scratch_shapes=[
            pltpu.VMEM((GROUPS, SLICE, PAGE), BF),
            pltpu.VMEM((CONVS, TURN, COLS), BF),
            pltpu.VMEM((HEADS_HERE, TURN, 128), F32),
            pltpu.VMEM((HEADS_HERE, TURN, 128), F32),
            pltpu.VMEM((HEADS_HERE, TURN, HS), F32),
            pltpu.VMEM((CHUNKS, TP, SLICE, 128), BF),
            pltpu.VMEM((GROUPS, 2, SLICE, PAGE), BF),
            pltpu.VMEM((GROUPS, 2, SLICE, PAGE), BF),
            pltpu.VMEM((WIDTH, 3 * COLS), BF),
            pltpu.VMEM((2 * PAGE, WIDTH), BF),
            pltpu.VMEM((CONVS, TURN, 3 * COLS), BF),
            pltpu.VMEM((CONVS, PREFIX, 2 * COLS), BF),
            pltpu.SemaphoreType.DMA((TURN_CHUNKS + 1,)),
            pltpu.SemaphoreType.DMA((CONVS,)),
            pltpu.SemaphoreType.DMA((3,)),
            pltpu.SemaphoreType.DMA((GROUPS,)),
            pltpu.SemaphoreType.DMA((GROUPS,)),
            pltpu.SemaphoreType.DMA((CHUNKS,)),
            pltpu.SemaphoreType.DMA((CHUNKS, 6)),
        ],
        compiler_params=pltpu.CompilerParams(
            collective_id=0, has_side_effects=True, vmem_limit_bytes=63 * 2**20
        ),
        cost_estimate=pl.CostEstimate(
            flops=27_000_000_000, bytes_accessed=26_000_000, transcendentals=1_600_000
        ),
        name="resume_attention",
    )(
        page_owner.T,
        prefix_len,
        turn_len,
        jnp.swapaxes(prefix_store, 1, 2),
        jnp.swapaxes(turn_rows, 1, 2),
        w_query,
        w_key,
        w_value,
    )


def solution(mesh):
    in_specs = (
        P("group", None, "tp"),
        P(),
        P("group"),
        P("group", None, "tp"),
        P("group"),
        P(None, "tp"),
        P(None, "tp"),
        P(None, "tp"),
    )
    out_specs = P("group", None, "tp")
    return jax.shard_map(body, mesh=mesh, in_specs=in_specs, out_specs=out_specs, check_vma=False)
```
